512 devices in a mesh: prow: 32 (over x, y), pcol: 16 (over z, core).
Axes of the slice: x: 4, y: 8, z: 8, core: 2. Of those that a mesh axis runs over, the one named last changes fastest.
Arguments:
- rhs_panel: float32 [2048, 2, 256], P(('prow', 'pcol')), may hold values from -6 to 6
- pivots: int32 [2048], replicated, may hold values from 0 to 2047, each once
- diag_inverse: float32 [2048, 2, 2048], P('pcol'), may hold values from -1 to 2, as said below
- panel_column: float32 [32768, 2, 2048], P('prow', None, 'pcol'), may hold values from -0.09375 to 0.09375
- trailing: float32 [32768, 2, 256], P(('prow', 'pcol')), may hold values from -6 to 6
- derivative: float32 [2048, 2, 256], P('pcol'), may hold values from -4 to 4
Outputs:
- updated: float32 [32768, 2, 256], P(('prow', 'pcol'))
- adjoint_panel: float32 [2048, 2, 256], P('pcol')
- sensitivity: float32 [256], replicated
The draws below stay inside these ranges and needn't reach their ends.
Inputs may be any that keep to these rules, and one draw needn't show every extreme that they name: `diag_inverse`: zero above the diagonal in both parts; diagonal real parts between 0.5 and 1.5. `pivots`: each of 0 to 2047 once.
All inputs are finite; a program needn't handle non-finite values.
Results may differ from the reference program's by a relative error of at most 0.00017.
Values sent between devices are 32-bit elements; how exact they have to be, the bound alone decides.
A program may use at most 64 MiB of HBM per device.

```python
import math
import jax
import jax.numpy as jnp
from jax import lax

NB = 2048
R = 256
ROWS = 32768


def draw_diag_inverse(key, part):
    key = jax.random.fold_in(key, 11)
    first, second, third = jax.random.split(key, 3)
    row_index = jnp.arange(NB)[:, None]
    col_index = jnp.arange(NB)[None, :]
    lower = row_index > col_index
    onside = row_index == col_index
    offdiag = jnp.clip(jax.random.normal(first, (NB, 2, NB), jnp.float32), -5.0, 5.0)
    diag_real = jax.random.uniform(second, (NB, NB), jnp.float32, 0.7, 1.3)
    diag_imag = jax.random.uniform(third, (NB, NB), jnp.float32, -0.3, 0.3)
    scale_off = 1.0 / math.sqrt(NB)
    real_part = jnp.where(lower, offdiag[:, 0, :] * scale_off, 0.0) + jnp.where(onside, diag_real, 0.0)
    imag_part = jnp.where(lower, offdiag[:, 1, :] * scale_off, 0.0) + jnp.where(onside, diag_imag, 0.0)
    return jnp.stack([real_part, imag_part], axis=1).astype(jnp.float32)


def draw_derivative(key, part):
    key = jax.random.fold_in(key, 12)
    first, second = jax.random.split(key, 2)
    rising = 1.0 + 2.0 * jnp.arange(NB, dtype=jnp.float32) / (NB - 1)
    rough = jnp.exp(jax.random.uniform(second, (NB,), jnp.float32, math.log(0.3), math.log(3.0)))
    values = jnp.clip(jax.random.normal(first, (NB, 2, R), jnp.float32), -5.0, 5.0)
    factor = rising * rough / math.sqrt(NB)
    return (values * factor[:, None, None]).astype(jnp.float32)


def block_scale(key, extent, cuts, smallest, top_value):
    gain = 1.0
    for position, shards_of in cuts:
        steps = jax.random.uniform(jax.random.fold_in(jax.random.fold_in(key, 6), position), (shards_of,), jnp.float32, smallest / len(cuts), top_value / len(cuts))
        gain = gain * jnp.repeat(jnp.exp(steps), extent[position] // shards_of).reshape((-1,) + (1,) * (len(extent) - 1 - position))
    return gain


def normal_values(rng, shape, scale, limit, shards=(), held_as=jnp.bfloat16):
    values = jax.random.normal(rng, shape, jnp.float32) * scale
    if len(shards) > 0:
        values = block_scale(rng, shape, shards, -0.22, 0.18) * values
    return jnp.clip(values, min=-limit, max=limit).astype(held_as)


def setup_inputs(seed: int = 0) -> dict:
    streams_of = jax.random.split(jax.random.key(seed), 7)
    return {
        "rhs_panel": normal_values(streams_of[0], (NB, 2, R), 1.0, 6.0, ((0, 512),), jnp.float32),
        "pivots": jax.random.permutation(streams_of[1], NB).astype(jnp.int32),
        "diag_inverse": draw_diag_inverse(jax.random.fold_in(streams_of[6], 71), 0),
        "panel_column": normal_values(streams_of[3], (ROWS, 2, NB), (2 * NB) ** -0.5, 0.09375, ((0, 32), (2, 16)), jnp.float32),
        "trailing": normal_values(streams_of[4], (ROWS, 2, R), 1.0, 6.0, ((0, 512),), jnp.float32),
        "derivative": draw_derivative(jax.random.fold_in(streams_of[6], 71), 0),
    }


def complex_product(lhs, rhs):
    count_rows = lhs.shape[0]
    inner = lhs.shape[2]
    flat = lhs.reshape(count_rows, 2 * inner)
    real_part = rhs[:, 0, :]
    imag_part = rhs[:, 1, :]
    stacked = jnp.concatenate([jnp.concatenate([real_part, imag_part], axis=1), jnp.concatenate([-imag_part, real_part], axis=1)], axis=0)
    result = jnp.dot(flat, stacked, preferred_element_type=jnp.float32, precision=lax.Precision.HIGHEST)
    return result.reshape(count_rows, 2, rhs.shape[2])


def reference(rhs_panel, pivots, diag_inverse, panel_column, trailing, derivative):
    ordered = jnp.take(rhs_panel, pivots, axis=0)
    adjoint_panel = complex_product(diag_inverse, ordered)
    updated = trailing - complex_product(panel_column, adjoint_panel)
    sensitivity = -jnp.sum(adjoint_panel * derivative, axis=(0, 1))
    return updated, adjoint_panel, sensitivity
```

```python
import functools

import jax
import jax.numpy as jnp
from jax import lax
from jax.experimental import pallas as pl
from jax.experimental.pallas import tpu as pltpu
from jax.sharding import PartitionSpec as P

NX = 4
LANES = 128
HALF = LANES // 2
F32 = jnp.float32
BF16 = jnp.bfloat16


def split(values):
    high = values.astype(BF16)
    return high, (values - high.astype(F32)).astype(BF16)


def dot(lhs, rhs, rhs_dim=0):
    return lax.dot_general(
        lhs, rhs, (((1,), (rhs_dim,)), ((), ())), preferred_element_type=F32
    )


def swap_halves(values):
    return pltpu.roll(values, HALF, 1)


def left_lanes(shape):
    return lax.broadcasted_iota(jnp.int32, shape, 1) < HALF


def turned(values):
    swapped = swap_halves(values)
    return jnp.where(left_lanes(values.shape), -swapped, swapped)


def three_pass(lhs_hi, lhs_lo, rhs):
    hi, lo = split(rhs)
    both = dot(lhs_hi, jnp.concatenate([hi, lo], axis=1))
    return (both[:, :LANES] + both[:, LANES:]) + dot(lhs_lo, hi)


def far_first(count):
    return sorted(range(1, count), key=lambda d: -min(d, count - d))


def kernel(
    ny, nz, rpd,
    rhs_in, piv_in, dinv_in, pc_in, tr_in, de_in,
    upd_out, adj_out, sens_out,
    rhs_v, swp_v, piv_v, dinv_v, pown, psib, tr_v, de_v,
    hsend, hrecv, gath, sel, vpart, rpart, sol, sib, lhs_hi, lhs_lo,
    prod, arrive, total, upd_v, adj_v, sens_v, sens_o, sens_x,
    load_sem, out_sem, ha_s, ha_r, ga_s, ga_r, rs_s, rs_r, ag_s,
    sx_s, s_r, t_r, p_s, p_r, ring_s, ring_r, u_s, u_r, ux_s, ux_r,
):
    row, col = lax.axis_index("prow"), lax.axis_index("pcol")
    x, y = row // ny, row % ny
    z, core = col // 2, col % 2
    other = z * 2 + 1 - core
    mb = dinv_v.shape[0] // (2 * piv_v.shape[0])
    tb = prod.shape[2]

    def remote(src, dst, send, recv, to_row, to_col):
        return pltpu.make_async_remote_copy(
            src_ref=src, dst_ref=dst, send_sem=send, recv_sem=recv,
            device_id=(to_row, to_col), device_id_type=pl.DeviceIdType.MESH,
        )

    def await_bytes(ref, sem):
        pltpu.make_async_copy(ref, ref, sem).wait()

    def along_x(d):
        return ((x + d) % NX) * ny + y

    def along_y(d):
        return x * ny + (y + d) % ny

    def along_z(d):
        return ((z + d + nz) % nz) * 2 + core

    barrier = pltpu.get_barrier_semaphore()

    def greet(to_row, to_col):
        pl.semaphore_signal(
            barrier, inc=1, device_id=(to_row, to_col), device_id_type=pl.DeviceIdType.MESH
        )

    z_line = [along_z(d) + flip for d in far_first(nz) for flip in (0, other - col)] + [other]
    for d in far_first(NX):
        greet(along_x(d), col)
    for to_col in z_line:
        greet(row, to_col)
    for d in far_first(ny):
        greet(along_y(d), col)

    loads = [
        pltpu.make_async_copy(src, dst, load_sem.at[n])
        for n, (src, dst) in enumerate([
            (rhs_in, rhs_v), (piv_in, piv_v), (dinv_in, dinv_v),
            (pc_in.at[:, core], pown), (de_in, de_v), (tr_in, tr_v),
        ])
    ]
    for load in loads[:3]:
        load.start()

    loads[0].wait()
    swp_v[...] = swap_halves(rhs_v[...])
    left = left_lanes((rpd, LANES))
    for s in range(NX):
        t, h = s // 2, s % 2
        re, im = pl.ds(2 * t, rpd, 4), pl.ds(2 * t + 1, rpd, 4)
        if h == 0:
            piece = jnp.where(left, rhs_v[re, :], swp_v[im, :])
        else:
            piece = jnp.where(left, swp_v[re, :], rhs_v[im, :])
        hsend[s, pl.ds(0, rpd)] = piece
        if rpd % 8:
            hsend[s, pl.ds(rpd, 8 - rpd % 8)] = jnp.zeros((8 - rpd % 8, LANES), F32)
    pl.semaphore_wait(barrier, NX - 1 + ny - 1 + 2 * nz - 1)

    for d in far_first(NX):
        remote(hsend.at[(x + d) % NX], hrecv.at[x], ha_s, ha_r, along_x(d), col).start()
    hrecv[x] = hsend[x]
    for load in loads[3:]:
        load.start()
    await_bytes(hrecv.at[pl.ds(0, NX - 1)], ha_r)
    for s in range(NX):
        gath[col, pl.ds(s * rpd, rpd)] = hrecv[s, pl.ds(0, rpd)]

    for to_col in z_line:
        remote(gath.at[col], gath.at[col], ga_s, ga_r, row, to_col).start()

    nq = 2 * nz * NX * rpd
    q = lax.broadcasted_iota(jnp.int32, (nq, 1), 0)
    wanted = rpd * (2 * nz * (ny * ((q // rpd) % NX) + y) + q // (NX * rpd)) + q % rpd
    wanted = jnp.broadcast_to(wanted, (nq, LANES))
    loads[1].wait()
    loads[2].wait()
    sel[...] = jnp.zeros(sel.shape, F32)
    tiles = piv_v.shape[0]

    @pl.loop(0, tiles // 2)
    def _(step):
        hot, high, low = [], [], []
        for half in range(2):
            t = step * 2 + half
            order = jnp.broadcast_to(piv_v[pl.ds(t, 1), :], (nq, LANES))
            hot.append(jnp.where(order == wanted, 1.0, 0.0).astype(BF16))
            parts = [
                split(dinv_v[pl.ds(t * 2 + c, mb, 2 * tiles), :]) for c in range(2)
            ]
            high.append(jnp.concatenate([parts[0][0], parts[1][0]], axis=0))
            low.append(jnp.concatenate([parts[0][1], parts[1][1]], axis=0))
        hots = jnp.concatenate(hot, axis=1)
        sel[0] += dot(jnp.concatenate(high, axis=1), hots, 1)
        sel[1] += dot(jnp.concatenate(low, axis=1), hots, 1)

    inv_hi = jnp.concatenate([sel[0, pl.ds(0, mb)], sel[0, pl.ds(mb, mb)]], axis=1).astype(BF16)
    inv_lo = jnp.concatenate([sel[1, pl.ds(0, mb)], sel[1, pl.ds(mb, mb)]], axis=1).astype(BF16)

    await_bytes(gath.at[pl.ds(0, 2 * nz - 1)], ga_r)
    rows = gath[...].reshape(nq, LANES)
    part = three_pass(inv_hi, inv_lo, jnp.concatenate([rows, turned(rows)], axis=0))
    vpart[...] = part.reshape(vpart.shape)

    for d in far_first(ny):
        remote(vpart.at[(y + d) % ny], rpart.at[y], rs_s, rs_r, along_y(d), col).start()
    rpart[y] = vpart[y]

    pshare = remote(pc_in.at[:, 1 - core], psib, p_s, p_r, row, other)
    pshare.start()

    away = (4, 3, 5, 2, 6, 1, 7, 0)

    def split_panel(src, lane):
        for n in range(nz):
            at = pl.ds(n * tb, tb)
            for c in range(2):
                hi, lo = split(src[(z + away[n]) % nz, pl.ds(c, tb, 2), :])
                lhs_hi[at, pl.ds(lane + c * LANES, LANES)] = hi
                lhs_lo[at, pl.ds(lane + c * LANES, LANES)] = lo

    loads[3].wait()
    split_panel(pown, 0)
    if ny > 1:
        await_bytes(rpart.at[pl.ds(0, ny - 1)], rs_r)
    sol[x, y] = functools.reduce(lambda a, b: a + b, [rpart[n] for n in range(ny)])

    plane = sorted(
        [(dx, dy) for dx in range(NX) for dy in range(ny) if dx or dy],
        key=lambda at: (at[0] > 0, -min(at[0], NX - at[0]) - min(at[1], ny - at[1])),
    )
    for dx, dy in plane:
        to_row = ((x + dx) % NX) * ny + (y + dy) % ny
        remote(sol.at[x, y], sol.at[x, y], ag_s.at[dx], s_r.at[x], to_row, col).start()
    pshare.wait_recv()
    split_panel(psib, 2 * LANES)

    def pass_on(k):
        s = (x + order[k]) % NX
        if k > 0:
            await_bytes(sol.at[s], s_r.at[s])
        elif ny > 1:
            await_bytes(sol.at[s, pl.ds(0, ny - 1)], s_r.at[s])
        copy = remote(sol.at[s], sib.at[s], sx_s.at[k], t_r.at[k], row, other)
        copy.start()
        return copy

    order = (0, 1, 3, 2)

    def leg(k, direction, slot):
        sign = 1 - 2 * direction
        block, hops = ((0, 2), (1 + direction, 1), (5 + direction, 1), (3 + direction, 2))[slot]
        at = pl.ds(direction * (tb // 2), tb // 2) if slot == 0 else pl.ds(0, tb)
        return at, remote(
            prod.at[k, block, at], arrive.at[k, direction, slot, at],
            ring_s.at[k, direction, slot], ring_r.at[k, direction, slot], row, along_z(sign * hops),
        )

    def product(k):
        s = (x + order[k]) % NX
        passed[k].wait_recv()
        own = sol[s].reshape(mb, LANES)
        sibling = sib[s].reshape(mb, LANES)
        rhs = jnp.concatenate([own, turned(own), sibling, turned(sibling)], axis=0)
        for first, count, slots in ((0, 3, (0, 1)), (3, 5, (2,))):
            at = pl.ds(first * tb, count * tb)
            block = three_pass(lhs_hi[at, :], lhs_lo[at, :], rhs)
            prod[k, pl.ds(first, count)] = block.reshape(count, tb, LANES)
            for slot in slots:
                for direction in range(2):
                    leg(k, direction, slot)[1].start()

    def middle(k):
        for direction in range(2):
            for slot in (0, 1):
                at, came = leg(k, direction, slot)
                came.wait_recv()
                prod[k, 3 + direction, at] += arrive[k, direction, slot, at]
            leg(k, direction, 3)[1].start()

    def finish(k):
        result = prod[k, 7]
        for direction in range(2):
            for slot in (2, 3):
                leg(k, direction, slot)[1].wait_recv()
                result = result + arrive[k, direction, slot]
        total[(x + order[k]) % NX] = result

    def unpack(first, second):
        mask = left_lanes(first.shape)
        return (
            jnp.where(mask, first, swap_halves(second)),
            jnp.where(mask, swap_halves(first), second),
        )

    adj_copy = pltpu.make_async_copy(adj_v, adj_out, out_sem.at[0])

    def panel_results():
        loads[4].wait()
        sens_v[z] = jnp.zeros(sens_v.shape[1:], F32)
        for t in range(2):
            parts = unpack(sol[2 * t].reshape(mb, LANES), sol[2 * t + 1].reshape(mb, LANES))
            acc = None
            for c in range(2):
                at = pl.ds(2 * t + c, mb, 4)
                adj_v[at, :] = parts[c]
                term = parts[c] * de_v[at, :]
                acc = term if acc is None else acc + term
            sens_v[z, pl.ds(t, 1)] = -jnp.sum(acc, axis=0, keepdims=True)
        for d in far_first(nz):
            remote(sens_v.at[z], sens_v.at[z], u_s, u_r, row, along_z(d)).start()
        adj_copy.start()

    passed = [pass_on(0)]
    product(0)
    passed += [pass_on(k) for k in range(1, NX)]
    product(1)
    middle(0)
    product(2)
    middle(1)
    product(3)
    middle(2)
    panel_results()
    middle(3)
    await_bytes(sens_v.at[pl.ds(0, nz - 1)], u_r)
    sens_o[...] = functools.reduce(lambda a, b: a + b, [sens_v[n] for n in range(nz)])
    sens_hand = remote(sens_o, sens_x, ux_s, ux_r, row, other)
    sens_hand.start()
    for k in range(NX):
        finish(k)

    loads[5].wait()
    for t in range(2):
        parts = unpack(total[2 * t], total[2 * t + 1])
        for c in range(2):
            at = pl.ds(2 * t + c, tb, 4)
            upd_v[at, :] = tr_v[at, :] - parts[c]
    upd_copy = pltpu.make_async_copy(upd_v, upd_out, out_sem.at[1])
    upd_copy.start()
    sens_hand.wait()
    sens_x[...] += sens_o[...]
    sens_copy = pltpu.make_async_copy(sens_x, sens_out, out_sem.at[2])
    sens_copy.start()

    await_bytes(hsend.at[pl.ds(0, NX - 1)], ha_s)
    await_bytes(gath.at[pl.ds(0, 2 * nz - 1)], ga_s)
    pshare.wait_send()
    if ny > 1:
        await_bytes(vpart.at[pl.ds(0, ny - 1)], rs_s)
        await_bytes(sol.at[0, pl.ds(0, ny - 1)], ag_s.at[0])
    for dx in range(1, NX):
        await_bytes(sol.at[dx], ag_s.at[dx])
    for copy in passed:
        copy.wait_send()
    for k in range(NX):
        for direction in range(2):
            for slot in range(4):
                leg(k, direction, slot)[1].wait_send()
    await_bytes(sens_v.at[pl.ds(0, nz - 1)], u_s)
    adj_copy.wait()
    upd_copy.wait()
    sens_copy.wait()


def rows_of_lanes(array):
    count, parts, width = array.shape
    tiles = width // LANES
    array = array.reshape(count, parts, tiles, LANES).transpose(0, 2, 1, 3)
    return array.reshape(count * tiles * parts, LANES)


def from_rows(array, count, tiles):
    return array.reshape(count, tiles, 2, LANES).transpose(0, 2, 1, 3).reshape(count, 2, tiles * LANES)


def make_per_device(prow, pcol):
    ny, nz = prow // NX, pcol // 2

    def per_device(rhs_panel, pivots, diag_inverse, panel_column, trailing, derivative):
        rpd = rhs_panel.shape[0]
        mb = diag_inverse.shape[0]
        tb = trailing.shape[0]
        nb = pivots.shape[0]
        vmem = lambda *shape: pltpu.VMEM(shape, F32)
        half = lambda *shape: pltpu.VMEM(shape, BF16)
        dma = lambda *shape: pltpu.SemaphoreType.DMA(shape) if shape else pltpu.SemaphoreType.DMA
        pad = -(-rpd // 8) * 8
        scratch = [
            vmem(rpd * 4, LANES), vmem(rpd * 4, LANES), pltpu.VMEM((nb // LANES, LANES), jnp.int32),
            vmem(mb * 2 * (nb // LANES), LANES),
            vmem(nz, 2 * tb, LANES), vmem(nz, 2 * tb, LANES),
            vmem(tb * 4, LANES), vmem(mb * 4, LANES),
            vmem(NX, pad, LANES), vmem(NX, pad, LANES), vmem(pcol, NX * rpd, LANES),
            vmem(2, 2 * mb, pcol * NX * rpd),
            vmem(ny, mb // ny, LANES), vmem(ny, mb // ny, LANES),
            vmem(NX, ny, mb // ny, LANES), vmem(NX, ny, mb // ny, LANES),
            half(nz * tb, 4 * LANES), half(nz * tb, 4 * LANES),
            vmem(NX, nz, tb, LANES), vmem(NX, 2, 4, tb, LANES), vmem(NX, tb, LANES),
            vmem(tb * 4, LANES), vmem(mb * 4, LANES), vmem(nz, 8, LANES), vmem(8, LANES), vmem(8, LANES),
            dma(6), dma(3), dma(), dma(), dma(), dma(), dma(), dma(), dma(NX),
            dma(NX), dma(NX), dma(NX), dma(), dma(), dma(NX, 2, 4), dma(NX, 2, 4), dma(), dma(), dma(), dma(),
        ]
        anywhere = pl.BlockSpec(memory_space=pltpu.HBM)
        updated, solved, sens = pl.pallas_call(
            functools.partial(kernel, ny, nz, rpd),
            out_shape=(
                jax.ShapeDtypeStruct((tb * 4, LANES), F32),
                jax.ShapeDtypeStruct((mb * 4, LANES), F32),
                jax.ShapeDtypeStruct((8, LANES), F32),
            ),
            in_specs=[anywhere] * 6,
            out_specs=(anywhere,) * 3,
            scratch_shapes=scratch,
            compiler_params=pltpu.CompilerParams(
                collective_id=0, has_side_effects=True, vmem_limit_bytes=48 * 1024 * 1024
            ),
            name="panel_step",
        )(*[pltpu.with_memory_space_constraint(operand, pltpu.HBM) for operand in (
            rows_of_lanes(rhs_panel),
            pivots.reshape(nb // LANES, LANES),
            rows_of_lanes(diag_inverse),
            rows_of_lanes(panel_column).reshape(nz, 2, 2 * tb, LANES),
            rows_of_lanes(trailing),
            rows_of_lanes(derivative),
        )])
        return from_rows(updated, tb, 2), from_rows(solved, mb, 2), sens[:2].reshape(2 * LANES)

    return per_device


def solution(mesh):
    in_specs = (
        P(("prow", "pcol"), None, None),
        P(),
        P("pcol", None, None),
        P("prow", None, "pcol"),
        P(("prow", "pcol"), None, None),
        P("pcol", None, None),
    )
    out_specs = (P(("prow", "pcol"), None, None), P("pcol", None, None), P())
    per_device = make_per_device(mesh.shape["prow"], mesh.shape["pcol"])
    return jax.shard_map(
        per_device, mesh=mesh, in_specs=in_specs, out_specs=out_specs, check_vma=False
    )
```

```python
import functools

import jax
import jax.numpy as jnp
from jax import lax
from jax.experimental import pallas as pl
from jax.experimental.pallas import tpu as pltpu
from jax.sharding import PartitionSpec as P

NX = 4
LANES = 128
HALF = LANES // 2
F32 = jnp.float32
BF16 = jnp.bfloat16


def split(values):
    high = values.astype(BF16)
    return high, (values - high.astype(F32)).astype(BF16)


def dot(lhs, rhs, rhs_dim=0):
    return lax.dot_general(
        lhs, rhs, (((1,), (rhs_dim,)), ((), ())), preferred_element_type=F32
    )


def swap_halves(values):
    return pltpu.roll(values, HALF, 1)


def left_lanes(shape):
    return lax.broadcasted_iota(jnp.int32, shape, 1) < HALF


def turned(values):
    swapped = swap_halves(values)
    return jnp.where(left_lanes(values.shape), -swapped, swapped)


def three_pass(lhs_hi, lhs_lo, rhs):
    hi, lo = split(rhs)
    both = dot(lhs_hi, jnp.concatenate([hi, lo], axis=1))
    return (both[:, :LANES] + both[:, LANES:]) + dot(lhs_lo, hi)


def far_first(count):
    return sorted(range(1, count), key=lambda d: -min(d, count - d))


def kernel(
    ny, nz, rpd,
    rhs_in, piv_in, dinv_in, pc_in, tr_in, de_in,
    upd_out, adj_out, sens_out,
    rhs_v, swp_v, piv_v, dinv_v, pown, psib, tr_v, de_v,
    hsend, hrecv, gath, sel, vpart, rpart, sol, sib, lhs_hi, lhs_lo,
    prod, arrive, total, upd_v, adj_v, sens_v, sens_o, sens_x,
    load_sem, out_sem, ha_s, ha_r, ga_s, ga_r, rs_s, rs_r, ag_s,
    sx_s, s_r, t_r, p_s, p_r, ring_s, ring_r, u_s, u_r, ux_s, ux_r,
):
    row, col = lax.axis_index("prow"), lax.axis_index("pcol")
    x, y = row // ny, row % ny
    z, core = col // 2, col % 2
    other = z * 2 + 1 - core
    mb = dinv_v.shape[0] // (2 * piv_v.shape[0])
    tb = prod.shape[2]

    def remote(src, dst, send, recv, to_row, to_col):
        return pltpu.make_async_remote_copy(
            src_ref=src, dst_ref=dst, send_sem=send, recv_sem=recv,
            device_id=(to_row, to_col), device_id_type=pl.DeviceIdType.MESH,
        )

    def await_bytes(ref, sem):
        pltpu.make_async_copy(ref, ref, sem).wait()

    def along_x(d):
        return ((x + d) % NX) * ny + y

    def along_y(d):
        return x * ny + (y + d) % ny

    def along_z(d):
        return ((z + d + nz) % nz) * 2 + core

    loads = [
        pltpu.make_async_copy(src, dst, load_sem.at[n])
        for n, (src, dst) in enumerate([
            (rhs_in, rhs_v), (piv_in, piv_v), (dinv_in, dinv_v),
            (pc_in.at[:, core], pown), (de_in, de_v), (tr_in, tr_v),
        ])
    ]
    for load in loads[:3]:
        load.start()

    barrier = pltpu.get_barrier_semaphore()

    def greet(to_row, to_col):
        pl.semaphore_signal(
            barrier, inc=1, device_id=(to_row, to_col), device_id_type=pl.DeviceIdType.MESH
        )

    z_line = [along_z(d) + flip for d in far_first(nz) for flip in (0, other - col)] + [other]
    for d in far_first(NX):
        greet(along_x(d), col)
    for to_col in z_line:
        greet(row, to_col)
    for d in far_first(ny):
        greet(along_y(d), col)

    loads[0].wait()
    swp_v[...] = swap_halves(rhs_v[...])
    left = left_lanes((rpd, LANES))
    for s in range(NX):
        t, h = s // 2, s % 2
        re, im = pl.ds(2 * t, rpd, 4), pl.ds(2 * t + 1, rpd, 4)
        if h == 0:
            piece = jnp.where(left, rhs_v[re, :], swp_v[im, :])
        else:
            piece = jnp.where(left, swp_v[re, :], rhs_v[im, :])
        hsend[s, pl.ds(0, rpd)] = piece
        if rpd % 8:
            hsend[s, pl.ds(rpd, 8 - rpd % 8)] = jnp.zeros((8 - rpd % 8, LANES), F32)
    pl.semaphore_wait(barrier, NX - 1 + ny - 1 + 2 * nz - 1)

    for d in far_first(NX):
        remote(hsend.at[(x + d) % NX], hrecv.at[x], ha_s, ha_r, along_x(d), col).start()
    hrecv[x] = hsend[x]
    for load in loads[3:]:
        load.start()

    nq = 2 * nz * NX * rpd
    q = lax.broadcasted_iota(jnp.int32, (nq, 1), 0)
    wanted = rpd * (2 * nz * (ny * ((q // rpd) % NX) + y) + q // (NX * rpd)) + q % rpd
    wanted = jnp.broadcast_to(wanted, (nq, LANES))
    loads[1].wait()
    loads[2].wait()
    sel[...] = jnp.zeros(sel.shape, F32)
    tiles = piv_v.shape[0]

    def pick(step):
        hot, high, low = [], [], []
        for half in range(2):
            t = step * 2 + half
            order = jnp.broadcast_to(piv_v[pl.ds(t, 1), :], (nq, LANES))
            hot.append(jnp.where(order == wanted, 1.0, 0.0).astype(BF16))
            parts = [
                split(dinv_v[pl.ds(t * 2 + c, mb, 2 * tiles), :]) for c in range(2)
            ]
            high.append(jnp.concatenate([parts[0][0], parts[1][0]], axis=0))
            low.append(jnp.concatenate([parts[0][1], parts[1][1]], axis=0))
        hots = jnp.concatenate(hot, axis=1)
        sel[0] += dot(jnp.concatenate(high, axis=1), hots, 1)
        sel[1] += dot(jnp.concatenate(low, axis=1), hots, 1)

    early = tiles // 2 * 3 // 8
    pl.loop(0, early)(pick)

    await_bytes(hrecv.at[pl.ds(0, NX - 1)], ha_r)
    for s in range(NX):
        gath[col, pl.ds(s * rpd, rpd)] = hrecv[s, pl.ds(0, rpd)]

    for to_col in z_line:
        remote(gath.at[col], gath.at[col], ga_s, ga_r, row, to_col).start()

    pl.loop(early, tiles // 2)(pick)
    inv_hi = jnp.concatenate([sel[0, pl.ds(0, mb)], sel[0, pl.ds(mb, mb)]], axis=1).astype(BF16)
    inv_lo = jnp.concatenate([sel[1, pl.ds(0, mb)], sel[1, pl.ds(mb, mb)]], axis=1).astype(BF16)

    await_bytes(gath.at[pl.ds(0, 2 * nz - 1)], ga_r)
    rows = gath[...].reshape(nq, LANES)
    part = three_pass(inv_hi, inv_lo, jnp.concatenate([rows, turned(rows)], axis=0))
    vpart[...] = part.reshape(vpart.shape)

    for d in far_first(ny):
        remote(vpart.at[(y + d) % ny], rpart.at[y], rs_s, rs_r, along_y(d), col).start()
    rpart[y] = vpart[y]

    pshare = remote(pc_in.at[:, 1 - core], psib, p_s, p_r, row, other)
    pshare.start()

    away = (4, 3, 5, 2, 6, 1, 7, 0)

    def split_panel(src, lane):
        for n in range(nz):
            at = pl.ds(n * tb, tb)
            for c in range(2):
                hi, lo = split(src[(z + away[n]) % nz, pl.ds(c, tb, 2), :])
                lhs_hi[at, pl.ds(lane + c * LANES, LANES)] = hi
                lhs_lo[at, pl.ds(lane + c * LANES, LANES)] = lo

    loads[3].wait()
    split_panel(pown, 0)
    if ny > 1:
        await_bytes(rpart.at[pl.ds(0, ny - 1)], rs_r)
    sol[row] = functools.reduce(lambda a, b: a + b, [rpart[n] for n in range(ny)])

    plane = sorted(
        [(dx, dy) for dx in range(NX) for dy in range(ny) if dx or dy],
        key=lambda at: (min(at[0], NX - at[0]), -min(at[1], ny - at[1])),
    )
    for dx, dy in plane:
        to_row = ((x + dx) % NX) * ny + (y + dy) % ny
        remote(sol.at[row], sol.at[row], ag_s, s_r.at[x], to_row, col).start()
    pshare.wait_recv()
    split_panel(psib, 2 * LANES)

    def pass_on(k):
        s = (x + order[k]) % NX
        line = pl.ds(s * ny, ny)
        if k > 0:
            await_bytes(sol.at[line], s_r.at[s])
        elif ny > 1:
            await_bytes(sol.at[pl.ds(s * ny, ny - 1)], s_r.at[s])
        copy = remote(sol.at[line], sib.at[line], sx_s, t_r.at[k], row, other)
        copy.start()
        return copy

    order = (0, 1, 3, 2)

    def leg(k, direction, slot):
        sign = 1 - 2 * direction
        block = (0, 1, 3, 5)[slot] + (direction if slot else 0)
        at = pl.ds(direction * (tb // 2), tb // 2) if slot == 0 else pl.ds(0, tb)
        return at, remote(
            prod.at[k, block, at], arrive.at[k, direction, slot, at],
            ring_s, ring_r.at[k, direction, max(slot, 1) - 1], row, along_z(sign * (1 if slot else 2)),
        )

    def came(k, direction, slot):
        if slot == 1:
            await_bytes(arrive.at[k, direction, pl.ds(0, 2), pl.ds(0, tb * 3 // 4)], ring_r.at[k, direction, 0])
        else:
            await_bytes(arrive.at[k, direction, slot], ring_r.at[k, direction, slot - 1])

    def advance(k, slot):
        for direction in range(2):
            if slot > 1:
                came(k, direction, slot - 1)
                block = (0, 1, 3, 5)[slot] + direction
                prod[k, block] += arrive[k, direction, slot - 1]
                if slot == 2:
                    at = leg(k, direction, 0)[0]
                    prod[k, block, at] += arrive[k, direction, 0, at]
            leg(k, direction, slot)[1].start()

    def finish(k):
        result = prod[k, 7]
        for direction in range(2):
            came(k, direction, 3)
            result = result + arrive[k, direction, 3]
        total[(x + order[k]) % NX] = result

    def slice_rows(ref, s):
        return ref[pl.ds(s * ny, ny)].reshape(mb, LANES)

    def panel_rhs(k):
        s = (x + order[k]) % NX
        passed[k].wait_recv()
        own, sibling = slice_rows(sol, s), slice_rows(sib, s)
        return jnp.concatenate([own, turned(own), sibling, turned(sibling)], axis=0)

    def product(k, rhs, first, count):
        at = pl.ds(first * tb, count * tb)
        block = three_pass(lhs_hi[at, :], lhs_lo[at, :], rhs)
        prod[k, pl.ds(first, count)] = block.reshape(count, tb, LANES)

    def unpack(first, second):
        mask = left_lanes(first.shape)
        return (
            jnp.where(mask, first, swap_halves(second)),
            jnp.where(mask, swap_halves(first), second),
        )

    adj_copy = pltpu.make_async_copy(adj_v, adj_out, out_sem.at[0])

    def panel_results():
        loads[4].wait()
        sens_v[z] = jnp.zeros(sens_v.shape[1:], F32)
        for t in range(2):
            parts = unpack(slice_rows(sol, 2 * t), slice_rows(sol, 2 * t + 1))
            acc = None
            for c in range(2):
                at = pl.ds(2 * t + c, mb, 4)
                adj_v[at, :] = parts[c]
                term = parts[c] * de_v[at, :]
                acc = term if acc is None else acc + term
            sens_v[z, pl.ds(t, 1)] = -jnp.sum(acc, axis=0, keepdims=True)
        for d in far_first(nz):
            remote(sens_v.at[z], sens_v.at[z], u_s, u_r, row, along_z(d)).start()
        adj_copy.start()

    passed = [pass_on(0)]
    rhs = []
    for k in range(NX):
        rhs.append(panel_rhs(k))
        product(k, rhs[k], 0, 3)
        advance(k, 0)
        advance(k, 1)
        if k == 0:
            product(0, rhs[0], 3, 5)
            passed += [pass_on(1), pass_on(2)]
        elif k == 1:
            passed.append(pass_on(3))
    for k in range(NX):
        if k > 0:
            product(k, rhs[k], 3, 5)
        advance(k, 2)
    panel_results()
    for k in range(NX):
        advance(k, 3)
    await_bytes(sens_v.at[pl.ds(0, nz - 1)], u_r)
    sens_o[...] = functools.reduce(lambda a, b: a + b, [sens_v[n] for n in range(nz)])
    sens_hand = remote(sens_o, sens_x, ux_s, ux_r, row, other)
    sens_hand.start()
    for k in range(NX):
        finish(k)

    loads[5].wait()
    for t in range(2):
        parts = unpack(total[2 * t], total[2 * t + 1])
        for c in range(2):
            at = pl.ds(2 * t + c, tb, 4)
            upd_v[at, :] = tr_v[at, :] - parts[c]
    upd_copy = pltpu.make_async_copy(upd_v, upd_out, out_sem.at[1])
    upd_copy.start()
    sens_hand.wait()
    sens_x[...] += sens_o[...]
    sens_copy = pltpu.make_async_copy(sens_x.at[pl.ds(0, 2)], sens_out, out_sem.at[2])
    sens_copy.start()

    await_bytes(hsend.at[pl.ds(0, NX - 1)], ha_s)
    await_bytes(gath.at[pl.ds(0, 2 * nz - 1)], ga_s)
    pshare.wait_send()
    if ny > 1:
        await_bytes(vpart.at[pl.ds(0, ny - 1)], rs_s)
    await_bytes(sol.at[pl.ds(0, NX * ny - 1)], ag_s)
    await_bytes(sol, sx_s)
    await_bytes(prod.at[:, pl.ds(0, nz - 1)], ring_s)
    await_bytes(sens_v.at[pl.ds(0, nz - 1)], u_s)
    adj_copy.wait()
    upd_copy.wait()
    sens_copy.wait()


def place(*refs):
    count = len(refs) // 2
    sems = refs[-1]
    copies = [
        pltpu.make_async_copy(refs[n], refs[count + n], sems.at[n]) for n in range(count)
    ]
    for copy in copies:
        copy.start()
    for copy in copies:
        copy.wait()


def rows_of_lanes(array):
    count, parts, width = array.shape
    tiles = width // LANES
    array = array.reshape(count, parts, tiles, LANES).transpose(0, 2, 1, 3)
    return array.reshape(count * tiles * parts, LANES)


def from_rows(array, count, tiles):
    return array.reshape(count, tiles, 2, LANES).transpose(0, 2, 1, 3).reshape(count, 2, tiles * LANES)


def make_per_device(prow, pcol):
    ny, nz = prow // NX, pcol // 2

    def per_device(rhs_panel, pivots, diag_inverse, panel_column, trailing, derivative):
        rpd = rhs_panel.shape[0]
        mb = diag_inverse.shape[0]
        tb = trailing.shape[0]
        nb = pivots.shape[0]
        vmem = lambda *shape: pltpu.VMEM(shape, F32)
        half = lambda *shape: pltpu.VMEM(shape, BF16)
        dma = lambda *shape: pltpu.SemaphoreType.DMA(shape) if shape else pltpu.SemaphoreType.DMA
        pad = -(-rpd // 8) * 8
        scratch = [
            vmem(rpd * 4, LANES), vmem(rpd * 4, LANES), pltpu.VMEM((nb // LANES, LANES), jnp.int32),
            vmem(mb * 2 * (nb // LANES), LANES),
            vmem(nz, 2 * tb, LANES), vmem(nz, 2 * tb, LANES),
            vmem(tb * 4, LANES), vmem(mb * 4, LANES),
            vmem(NX, pad, LANES), vmem(NX, pad, LANES), vmem(pcol, NX * rpd, LANES),
            vmem(2, 2 * mb, pcol * NX * rpd),
            vmem(ny, mb // ny, LANES), vmem(ny, mb // ny, LANES),
            vmem(NX * ny, mb // ny, LANES), vmem(NX * ny, mb // ny, LANES),
            half(nz * tb, 4 * LANES), half(nz * tb, 4 * LANES),
            vmem(NX, nz, tb, LANES), vmem(NX, 2, 4, tb, LANES), vmem(NX, tb, LANES),
            vmem(tb * 4, LANES), vmem(mb * 4, LANES), vmem(nz, 8, LANES), vmem(8, LANES), vmem(8, LANES),
            dma(6), dma(3), dma(), dma(), dma(), dma(), dma(), dma(), dma(),
            dma(), dma(NX), dma(NX), dma(), dma(), dma(), dma(NX, 2, 3), dma(), dma(), dma(), dma(),
        ]
        anywhere = pl.BlockSpec(memory_space=pltpu.HBM)
        updated, solved, sens = pl.pallas_call(
            functools.partial(kernel, ny, nz, rpd),
            out_shape=(
                jax.ShapeDtypeStruct((tb * 4, LANES), F32),
                jax.ShapeDtypeStruct((mb * 4, LANES), F32),
                jax.ShapeDtypeStruct((2, LANES), F32),
            ),
            in_specs=[anywhere] * 6,
            out_specs=(anywhere,) * 3,
            scratch_shapes=scratch,
            compiler_params=pltpu.CompilerParams(
                collective_id=0, has_side_effects=True, vmem_limit_bytes=48 * 1024 * 1024
            ),
            name="panel_step",
        )(*[pltpu.with_memory_space_constraint(operand, pltpu.HBM) for operand in (
            rows_of_lanes(rhs_panel),
            pivots.reshape(nb // LANES, LANES),
            rows_of_lanes(diag_inverse),
            rows_of_lanes(panel_column).reshape(nz, 2, 2 * tb, LANES),
            rows_of_lanes(trailing),
            rows_of_lanes(derivative),
        )])
        updated, solved, sens = pl.pallas_call(
            place,
            out_shape=(
                jax.ShapeDtypeStruct(updated.shape, F32),
                jax.ShapeDtypeStruct(solved.shape, F32),
                jax.ShapeDtypeStruct(sens.shape, F32),
            ),
            in_specs=[pl.BlockSpec(memory_space=pltpu.VMEM)] * 3,
            out_specs=(pl.BlockSpec(memory_space=pltpu.HBM),) * 3,
            scratch_shapes=[pltpu.SemaphoreType.DMA((3,))],
            name="place_results",
        )(*[
            pltpu.with_memory_space_constraint(result, pltpu.VMEM)
            for result in (updated, solved, sens)
        ])
        return from_rows(updated, tb, 2), from_rows(solved, mb, 2), sens.reshape(2 * LANES)

    return per_device


def solution(mesh):
    in_specs = (
        P(("prow", "pcol"), None, None),
        P(),
        P("pcol", None, None),
        P("prow", None, "pcol"),
        P(("prow", "pcol"), None, None),
        P("pcol", None, None),
    )
    out_specs = (P(("prow", "pcol"), None, None), P("pcol", None, None), P())
    per_device = make_per_device(mesh.shape["prow"], mesh.shape["pcol"])
    return jax.shard_map(
        per_device, mesh=mesh, in_specs=in_specs, out_specs=out_specs, check_vma=False
    )
```

```python
import functools

import jax
import jax.numpy as jnp
from jax import lax
from jax.experimental import pallas as pl
from jax.experimental.pallas import tpu as pltpu
from jax.sharding import PartitionSpec as P

NX = 4
LANES = 128
HALF = LANES // 2
F32 = jnp.float32
BF16 = jnp.bfloat16


def split(values):
    high = values.astype(BF16)
    return high, (values - high.astype(F32)).astype(BF16)


def dot(lhs, rhs, rhs_dim=0):
    return lax.dot_general(
        lhs, rhs, (((1,), (rhs_dim,)), ((), ())), preferred_element_type=F32
    )


def swap_halves(values):
    return pltpu.roll(values, HALF, 1)


def left_lanes(shape):
    return lax.broadcasted_iota(jnp.int32, shape, 1) < HALF


def turned(values):
    swapped = swap_halves(values)
    return jnp.where(left_lanes(values.shape), -swapped, swapped)


def three_pass(lhs_hi, lhs_lo, rhs):
    hi, lo = split(rhs)
    both = dot(lhs_hi, jnp.concatenate([hi, lo], axis=1))
    return (both[:, :LANES] + both[:, LANES:]) + dot(lhs_lo, hi)


def far_first(count):
    return sorted(range(1, count), key=lambda d: -min(d, count - d))


def kernel(
    ny, nz, rpd,
    rhs_in, piv_in, dinv_in, pc_in, tr_in, de_in,
    upd_out, adj_out, sens_out,
    rhs_v, swp_v, piv_v, dinv_v, pown, psib, tr_v, de_v,
    hsend, hrecv, gath, sel, vpart, rpart, sol, sib, lhs_hi, lhs_lo,
    prod, arrive, total, upd_v, adj_v, sens_v, sens_o, sens_x,
    load_sem, out_sem, ha_s, ha_r, ga_s, ga_r, rs_s, rs_r, ag_s,
    sx_s, s_r, t_r, p_s, p_r, ring_s, ring_r, u_s, u_r, ux_s, ux_r,
):
    row, col = lax.axis_index("prow"), lax.axis_index("pcol")
    x, y = row // ny, row % ny
    z, core = col // 2, col % 2
    other = z * 2 + 1 - core
    mb = dinv_v.shape[0] // (2 * piv_v.shape[0])
    tb = prod.shape[2]

    def remote(src, dst, send, recv, to_row, to_col):
        return pltpu.make_async_remote_copy(
            src_ref=src, dst_ref=dst, send_sem=send, recv_sem=recv,
            device_id=(to_row, to_col), device_id_type=pl.DeviceIdType.MESH,
        )

    def await_bytes(ref, sem):
        pltpu.make_async_copy(ref, ref, sem).wait()

    def along_x(d):
        return ((x + d) % NX) * ny + y

    def along_y(d):
        return x * ny + (y + d) % ny

    def along_z(d):
        return ((z + d + nz) % nz) * 2 + core

    loads = [
        pltpu.make_async_copy(src, dst, load_sem.at[n])
        for n, (src, dst) in enumerate([
            (rhs_in, rhs_v), (piv_in, piv_v), (dinv_in, dinv_v),
            (pc_in.at[:, core], pown), (de_in, de_v), (tr_in, tr_v),
        ])
    ]
    for load in loads[:3]:
        load.start()

    barrier = pltpu.get_barrier_semaphore()

    def greet(to_row, to_col):
        pl.semaphore_signal(
            barrier, inc=1, device_id=(to_row, to_col), device_id_type=pl.DeviceIdType.MESH
        )

    z_line = [along_z(d) + flip for d in far_first(nz) for flip in (0, other - col)] + [other]
    for d in far_first(NX):
        greet(along_x(d), col)
    for to_col in z_line:
        greet(row, to_col)
    for d in far_first(ny):
        greet(along_y(d), col)

    loads[0].wait()
    swp_v[...] = swap_halves(rhs_v[...])
    left = left_lanes((rpd, LANES))
    for s in range(NX):
        t, h = s // 2, s % 2
        re, im = pl.ds(2 * t, rpd, 4), pl.ds(2 * t + 1, rpd, 4)
        if h == 0:
            piece = jnp.where(left, rhs_v[re, :], swp_v[im, :])
        else:
            piece = jnp.where(left, swp_v[re, :], rhs_v[im, :])
        hsend[s, pl.ds(0, rpd)] = piece
        if rpd % 8:
            hsend[s, pl.ds(rpd, 8 - rpd % 8)] = jnp.zeros((8 - rpd % 8, LANES), F32)
    pl.semaphore_wait(barrier, NX - 1 + ny - 1 + 2 * nz - 1)

    for d in far_first(NX):
        remote(hsend.at[(x + d) % NX], hrecv.at[x], ha_s, ha_r, along_x(d), col).start()
    hrecv[x] = hsend[x]
    for load in loads[3:]:
        load.start()

    nq = 2 * nz * NX * rpd
    q = lax.broadcasted_iota(jnp.int32, (nq, 1), 0)
    wanted = rpd * (2 * nz * (ny * ((q // rpd) % NX) + y) + q // (NX * rpd)) + q % rpd
    wanted = jnp.broadcast_to(wanted, (nq, LANES))
    loads[1].wait()
    loads[2].wait()
    sel[...] = jnp.zeros(sel.shape, F32)
    tiles = piv_v.shape[0]

    def pick(step):
        hot, high, low = [], [], []
        for half in range(2):
            t = step * 2 + half
            order = jnp.broadcast_to(piv_v[pl.ds(t, 1), :], (nq, LANES))
            hot.append(jnp.where(order == wanted, 1.0, 0.0).astype(BF16))
            parts = [
                split(dinv_v[pl.ds(t * 2 + c, mb, 2 * tiles), :]) for c in range(2)
            ]
            high.append(jnp.concatenate([parts[0][0], parts[1][0]], axis=0))
            low.append(jnp.concatenate([parts[0][1], parts[1][1]], axis=0))
        hots = jnp.concatenate(hot, axis=1)
        sel[0] += dot(jnp.concatenate(high, axis=1), hots, 1)
        sel[1] += dot(jnp.concatenate(low, axis=1), hots, 1)

    early = tiles // 2 * 3 // 8
    pl.loop(0, early)(pick)

    await_bytes(hrecv.at[pl.ds(0, NX - 1)], ha_r)
    for s in range(NX):
        gath[col, pl.ds(s * rpd, rpd)] = hrecv[s, pl.ds(0, rpd)]

    for to_col in z_line:
        remote(gath.at[col], gath.at[col], ga_s, ga_r, row, to_col).start()

    pl.loop(early, tiles // 2)(pick)
    inv_hi = jnp.concatenate([sel[0, pl.ds(0, mb)], sel[0, pl.ds(mb, mb)]], axis=1).astype(BF16)
    inv_lo = jnp.concatenate([sel[1, pl.ds(0, mb)], sel[1, pl.ds(mb, mb)]], axis=1).astype(BF16)

    await_bytes(gath.at[pl.ds(0, 2 * nz - 1)], ga_r)
    rows = gath[...].reshape(nq, LANES)
    part = three_pass(inv_hi, inv_lo, jnp.concatenate([rows, turned(rows)], axis=0))
    vpart[...] = part.reshape(vpart.shape)

    for d in far_first(ny):
        remote(vpart.at[(y + d) % ny], rpart.at[y], rs_s, rs_r, along_y(d), col).start()
    rpart[y] = vpart[y]

    pshare = remote(pc_in.at[:, 1 - core], psib, p_s, p_r, row, other)
    pshare.start()

    away = (4, 3, 5, 2, 6, 1, 7, 0)

    def split_panel(src, lane):
        for n in range(nz):
            at = pl.ds(n * tb, tb)
            for c in range(2):
                hi, lo = split(src[(z + away[n]) % nz, pl.ds(c, tb, 2), :])
                lhs_hi[at, pl.ds(lane + c * LANES, LANES)] = hi
                lhs_lo[at, pl.ds(lane + c * LANES, LANES)] = lo

    loads[3].wait()
    split_panel(pown, 0)
    if ny > 1:
        await_bytes(rpart.at[pl.ds(0, ny - 1)], rs_r)
    sol[row] = functools.reduce(lambda a, b: a + b, [rpart[n] for n in range(ny)])

    plane = sorted(
        [(dx, dy) for dx in range(NX) for dy in range(ny) if dx or dy],
        key=lambda at: (min(at[0], NX - at[0]), -min(at[1], ny - at[1])),
    )
    for dx, dy in plane:
        to_row = ((x + dx) % NX) * ny + (y + dy) % ny
        remote(sol.at[row], sol.at[row], ag_s, s_r.at[x], to_row, col).start()
    pshare.wait_recv()
    split_panel(psib, 2 * LANES)

    def pass_on(k):
        s = (x + order[k]) % NX
        line = pl.ds(s * ny, ny)
        if k > 0:
            await_bytes(sol.at[line], s_r.at[s])
        elif ny > 1:
            await_bytes(sol.at[pl.ds(s * ny, ny - 1)], s_r.at[s])
        copy = remote(sol.at[line], sib.at[line], sx_s, t_r.at[k], row, other)
        copy.start()
        return copy

    order = (0, 1, 3, 2)

    def leg(k, direction, slot):
        sign = 1 - 2 * direction
        block = (0, 1, 3, 5)[slot] + (direction if slot else 0)
        at = pl.ds(direction * (tb // 2), tb // 2) if slot == 0 else pl.ds(0, tb)
        return at, remote(
            prod.at[k, block, at], arrive.at[k, direction, slot, at],
            ring_s, ring_r.at[k, direction, max(slot, 1) - 1], row, along_z(sign * (1 if slot else 2)),
        )

    def came(k, direction, slot):
        if slot == 1:
            await_bytes(arrive.at[k, direction, pl.ds(0, 2), pl.ds(0, tb * 3 // 4)], ring_r.at[k, direction, 0])
        else:
            await_bytes(arrive.at[k, direction, slot], ring_r.at[k, direction, slot - 1])

    def advance(k, slot):
        for direction in range(2):
            if slot > 1:
                came(k, direction, slot - 1)
                block = (0, 1, 3, 5)[slot] + direction
                prod[k, block] += arrive[k, direction, slot - 1]
                if slot == 2:
                    at = leg(k, direction, 0)[0]
                    prod[k, block, at] += arrive[k, direction, 0, at]
            leg(k, direction, slot)[1].start()

    def finish(k):
        result = prod[k, 7]
        for direction in range(2):
            came(k, direction, 3)
            result = result + arrive[k, direction, 3]
        total[(x + order[k]) % NX] = result

    def slice_rows(ref, s):
        return ref[pl.ds(s * ny, ny)].reshape(mb, LANES)

    def panel_rhs(k):
        s = (x + order[k]) % NX
        passed[k].wait_recv()
        own, sibling = slice_rows(sol, s), slice_rows(sib, s)
        return jnp.concatenate([own, turned(own), sibling, turned(sibling)], axis=0)

    def product(k, rhs, first, count):
        at = pl.ds(first * tb, count * tb)
        block = three_pass(lhs_hi[at, :], lhs_lo[at, :], rhs)
        prod[k, pl.ds(first, count)] = block.reshape(count, tb, LANES)

    def unpack(first, second):
        mask = left_lanes(first.shape)
        return (
            jnp.where(mask, first, swap_halves(second)),
            jnp.where(mask, swap_halves(first), second),
        )

    adj_copy = pltpu.make_async_copy(adj_v, adj_out, out_sem.at[0])

    def panel_results():
        loads[4].wait()
        for t in range(2):
            parts = unpack(slice_rows(sol, 2 * t), slice_rows(sol, 2 * t + 1))
            acc = None
            for c in range(2):
                at = pl.ds(2 * t + c, mb, 4)
                adj_v[at, :] = parts[c]
                term = parts[c] * de_v[at, :]
                acc = term if acc is None else acc + term
            sens_v[z, pl.ds(t, 1)] = -jnp.sum(acc, axis=0, keepdims=True)
        for d in far_first(nz):
            remote(sens_v.at[z], sens_v.at[z], u_s, u_r, row, along_z(d)).start()
        adj_copy.start()

    passed = [pass_on(0)]
    rhs = []

    def lead(k):
        rhs.append(panel_rhs(k))
        product(k, rhs[k], 0, 3)
        advance(k, 0)
        advance(k, 1)

    def trail(k):
        product(k, rhs[k], 3, 5)

    lead(0)
    trail(0)
    passed += [pass_on(1), pass_on(2)]
    lead(1)
    lead(2)
    passed.append(pass_on(3))
    trail(1)
    trail(2)
    lead(3)
    advance(0, 2)
    trail(3)
    panel_results()
    for k in range(1, NX):
        advance(k, 2)
    for k in range(NX):
        advance(k, 3)
    await_bytes(sens_v.at[pl.ds(0, nz - 1)], u_r)
    sens_o[...] = functools.reduce(lambda a, b: a + b, [sens_v[n] for n in range(nz)])
    sens_hand = remote(sens_o, sens_x, ux_s, ux_r, row, other)
    sens_hand.start()
    for k in range(NX):
        finish(k)

    loads[5].wait()
    for t in range(2):
        parts = unpack(total[2 * t], total[2 * t + 1])
        for c in range(2):
            at = pl.ds(2 * t + c, tb, 4)
            upd_v[at, :] = tr_v[at, :] - parts[c]
    upd_copy = pltpu.make_async_copy(upd_v, upd_out, out_sem.at[1])
    upd_copy.start()
    sens_hand.wait()
    sens_x[...] += sens_o[...]
    sens_copy = pltpu.make_async_copy(sens_x, sens_out, out_sem.at[2])
    sens_copy.start()

    await_bytes(hsend.at[pl.ds(0, NX - 1)], ha_s)
    await_bytes(gath.at[pl.ds(0, 2 * nz - 1)], ga_s)
    pshare.wait_send()
    if ny > 1:
        await_bytes(vpart.at[pl.ds(0, ny - 1)], rs_s)
    await_bytes(sol.at[pl.ds(0, NX * ny - 1)], ag_s)
    await_bytes(sol, sx_s)
    await_bytes(prod.at[:, pl.ds(0, nz - 1)], ring_s)
    await_bytes(sens_v.at[pl.ds(0, nz - 1)], u_s)
    adj_copy.wait()
    upd_copy.wait()
    sens_copy.wait()


def place(*refs):
    count = len(refs) // 2
    sems = refs[-1]
    copies = [
        pltpu.make_async_copy(refs[n], refs[count + n], sems.at[n]) for n in range(count)
    ]
    for copy in copies:
        copy.start()
    for copy in copies:
        copy.wait()


def rows_of_lanes(array):
    count, parts, width = array.shape
    tiles = width // LANES
    array = array.reshape(count, parts, tiles, LANES).transpose(0, 2, 1, 3)
    return array.reshape(count * tiles * parts, LANES)


def from_rows(array, count, tiles):
    return array.reshape(count, tiles, 2, LANES).transpose(0, 2, 1, 3).reshape(count, 2, tiles * LANES)


def make_per_device(prow, pcol):
    ny, nz = prow // NX, pcol // 2

    def per_device(rhs_panel, pivots, diag_inverse, panel_column, trailing, derivative):
        rpd = rhs_panel.shape[0]
        mb = diag_inverse.shape[0]
        tb = trailing.shape[0]
        nb = pivots.shape[0]
        vmem = lambda *shape: pltpu.VMEM(shape, F32)
        half = lambda *shape: pltpu.VMEM(shape, BF16)
        dma = lambda *shape: pltpu.SemaphoreType.DMA(shape) if shape else pltpu.SemaphoreType.DMA
        pad = -(-rpd // 8) * 8
        scratch = [
            vmem(rpd * 4, LANES), vmem(rpd * 4, LANES), pltpu.VMEM((nb // LANES, LANES), jnp.int32),
            vmem(mb * 2 * (nb // LANES), LANES),
            vmem(nz, 2 * tb, LANES), vmem(nz, 2 * tb, LANES),
            vmem(tb * 4, LANES), vmem(mb * 4, LANES),
            vmem(NX, pad, LANES), vmem(NX, pad, LANES), vmem(pcol, NX * rpd, LANES),
            vmem(2, 2 * mb, pcol * NX * rpd),
            vmem(ny, mb // ny, LANES), vmem(ny, mb // ny, LANES),
            vmem(NX * ny, mb // ny, LANES), vmem(NX * ny, mb // ny, LANES),
            half(nz * tb, 4 * LANES), half(nz * tb, 4 * LANES),
            vmem(NX, nz, tb, LANES), vmem(NX, 2, 4, tb, LANES), vmem(NX, tb, LANES),
            vmem(tb * 4, LANES), vmem(mb * 4, LANES), vmem(nz, 2, LANES), vmem(2, LANES), vmem(2, LANES),
            dma(6), dma(3), dma(), dma(), dma(), dma(), dma(), dma(), dma(),
            dma(), dma(NX), dma(NX), dma(), dma(), dma(), dma(NX, 2, 3), dma(), dma(), dma(), dma(),
        ]
        anywhere = pl.BlockSpec(memory_space=pltpu.HBM)
        updated, solved, sens = pl.pallas_call(
            functools.partial(kernel, ny, nz, rpd),
            out_shape=(
                jax.ShapeDtypeStruct((tb * 4, LANES), F32),
                jax.ShapeDtypeStruct((mb * 4, LANES), F32),
                jax.ShapeDtypeStruct((2, LANES), F32),
            ),
            in_specs=[anywhere] * 6,
            out_specs=(anywhere,) * 3,
            scratch_shapes=scratch,
            compiler_params=pltpu.CompilerParams(
                collective_id=0, has_side_effects=True, vmem_limit_bytes=48 * 1024 * 1024
            ),
            name="panel_step",
        )(*[pltpu.with_memory_space_constraint(operand, pltpu.HBM) for operand in (
            rows_of_lanes(rhs_panel),
            pivots.reshape(nb // LANES, LANES),
            rows_of_lanes(diag_inverse),
            rows_of_lanes(panel_column).reshape(nz, 2, 2 * tb, LANES),
            rows_of_lanes(trailing),
            rows_of_lanes(derivative),
        )])
        updated, solved, sens = pl.pallas_call(
            place,
            out_shape=(
                jax.ShapeDtypeStruct(updated.shape, F32),
                jax.ShapeDtypeStruct(solved.shape, F32),
                jax.ShapeDtypeStruct(sens.shape, F32),
            ),
            in_specs=[pl.BlockSpec(memory_space=pltpu.VMEM)] * 3,
            out_specs=(pl.BlockSpec(memory_space=pltpu.HBM),) * 3,
            scratch_shapes=[pltpu.SemaphoreType.DMA((3,))],
            name="place_results",
        )(*[
            pltpu.with_memory_space_constraint(result, pltpu.VMEM)
            for result in (updated, solved, sens)
        ])
        return from_rows(updated, tb, 2), from_rows(solved, mb, 2), sens.reshape(2 * LANES)

    return per_device


def solution(mesh):
    in_specs = (
        P(("prow", "pcol"), None, None),
        P(),
        P("pcol", None, None),
        P("prow", None, "pcol"),
        P(("prow", "pcol"), None, None),
        P("pcol", None, None),
    )
    out_specs = (P(("prow", "pcol"), None, None), P("pcol", None, None), P())
    per_device = make_per_device(mesh.shape["prow"], mesh.shape["pcol"])
    return jax.shard_map(
        per_device, mesh=mesh, in_specs=in_specs, out_specs=out_specs, check_vma=False
    )
```

```python
import functools

import jax
import jax.numpy as jnp
from jax import lax
from jax.experimental import pallas as pl
from jax.experimental.pallas import tpu as pltpu
from jax.sharding import PartitionSpec as P

NX = 4
LANES = 128
HALF = LANES // 2
F32 = jnp.float32
BF16 = jnp.bfloat16


def split(values):
    high = values.astype(BF16)
    return high, (values - high.astype(F32)).astype(BF16)


def dot(lhs, rhs, rhs_dim=0):
    return lax.dot_general(
        lhs, rhs, (((1,), (rhs_dim,)), ((), ())), preferred_element_type=F32
    )


def swap_halves(values):
    return pltpu.roll(values, HALF, 1)


def left_lanes(shape):
    return lax.broadcasted_iota(jnp.int32, shape, 1) < HALF


def turned(values):
    swapped = swap_halves(values)
    return jnp.where(left_lanes(values.shape), -swapped, swapped)


def three_pass(lhs_hi, lhs_lo, rhs):
    hi, lo = split(rhs)
    both = dot(lhs_hi, jnp.concatenate([hi, lo], axis=1))
    return (both[:, :LANES] + both[:, LANES:]) + dot(lhs_lo, hi)


def far_first(count):
    return sorted(range(1, count), key=lambda d: -min(d, count - d))


def kernel(
    ny, nz, rpd,
    rhs_in, piv_in, dinv_in, pc_in, tr_in, de_in,
    upd_out, adj_out, sens_out,
    rhs_v, swp_v, piv_v, dinv_v, pown, psib, de_v,
    hsend, hrecv, gath, sel, vpart, rpart, sol, sib, lhs_hi, lhs_lo,
    prod, arrive, upd_v, adj_v, sens_v, sens_o, sens_x,
    load_sem, out_sem, ha_r, ga_r, rs_r, s_r, t_r, p_s, p_r, ring_r, u_r, ux_r, sent_sem,
):
    row, col = lax.axis_index("prow"), lax.axis_index("pcol")
    x, y = row // ny, row % ny
    z, core = col // 2, col % 2
    other = z * 2 + 1 - core
    mb = dinv_v.shape[0] // (2 * piv_v.shape[0])
    tb = prod.shape[2]

    def remote(src, dst, send, recv, to_row, to_col):
        return pltpu.make_async_remote_copy(
            src_ref=src, dst_ref=dst, send_sem=send, recv_sem=recv,
            device_id=(to_row, to_col), device_id_type=pl.DeviceIdType.MESH,
        )

    def await_bytes(ref, sem):
        pltpu.make_async_copy(ref, ref, sem).wait()

    def along_x(d):
        return ((x + d) % NX) * ny + y

    def along_y(d):
        return x * ny + (y + d) % ny

    def along_z(d):
        return ((z + d + nz) % nz) * 2 + core

    loads = [
        pltpu.make_async_copy(src, dst, load_sem.at[n])
        for n, (src, dst) in enumerate([
            (rhs_in, rhs_v), (piv_in, piv_v), (dinv_in, dinv_v),
            (pc_in.at[:, core], pown), (de_in, de_v), (tr_in, upd_v),
        ])
    ]
    for load in loads[:3]:
        load.start()

    barrier = pltpu.get_barrier_semaphore()

    def greet(to_row, to_col):
        pl.semaphore_signal(
            barrier, inc=1, device_id=(to_row, to_col), device_id_type=pl.DeviceIdType.MESH
        )

    z_line = [along_z(d) + flip for d in far_first(nz) for flip in (0, other - col)] + [other]
    for d in far_first(NX):
        greet(along_x(d), col)
    for to_col in z_line:
        greet(row, to_col)
    for d in far_first(ny):
        greet(along_y(d), col)

    loads[0].wait()
    swp_v[...] = swap_halves(rhs_v[...])
    left = left_lanes((rpd, LANES))
    for s in range(NX):
        t, h = s // 2, s % 2
        re, im = pl.ds(2 * t, rpd, 4), pl.ds(2 * t + 1, rpd, 4)
        if h == 0:
            piece = jnp.where(left, rhs_v[re, :], swp_v[im, :])
        else:
            piece = jnp.where(left, swp_v[re, :], rhs_v[im, :])
        hsend[s, pl.ds(0, rpd)] = piece
        if rpd % 8:
            hsend[s, pl.ds(rpd, 8 - rpd % 8)] = jnp.zeros((8 - rpd % 8, LANES), F32)
    pl.semaphore_wait(barrier, NX - 1 + ny - 1 + 2 * nz - 1)

    for d in far_first(NX):
        remote(hsend.at[(x + d) % NX], hrecv.at[x], sent_sem, ha_r, along_x(d), col).start()
    hrecv[x] = hsend[x]
    for load in loads[3:]:
        load.start()

    nq = 2 * nz * NX * rpd
    q = lax.broadcasted_iota(jnp.int32, (nq, 1), 0)
    wanted = rpd * (2 * nz * (ny * ((q // rpd) % NX) + y) + q // (NX * rpd)) + q % rpd
    wanted = jnp.broadcast_to(wanted, (nq, LANES))
    loads[1].wait()
    loads[2].wait()
    sel[...] = jnp.zeros(sel.shape, F32)
    tiles = piv_v.shape[0]

    def pick(step):
        hot, high, low = [], [], []
        for half in range(2):
            t = step * 2 + half
            order = jnp.broadcast_to(piv_v[pl.ds(t, 1), :], (nq, LANES))
            hot.append(jnp.where(order == wanted, 1.0, 0.0).astype(BF16))
            parts = [
                split(dinv_v[pl.ds(t * 2 + c, mb, 2 * tiles), :]) for c in range(2)
            ]
            high.append(jnp.concatenate([parts[0][0], parts[1][0]], axis=0))
            low.append(jnp.concatenate([parts[0][1], parts[1][1]], axis=0))
        hots = jnp.concatenate(hot, axis=1)
        sel[0] += dot(jnp.concatenate(high, axis=1), hots, 1)
        sel[1] += dot(jnp.concatenate(low, axis=1), hots, 1)

    early = tiles // 2 * 3 // 8
    pl.loop(0, early)(pick)

    await_bytes(hrecv.at[pl.ds(0, NX - 1)], ha_r)
    for s in range(NX):
        gath[col, pl.ds(s * rpd, rpd)] = hrecv[s, pl.ds(0, rpd)]

    for to_col in z_line:
        remote(gath.at[col], gath.at[col], sent_sem, ga_r, row, to_col).start()

    pl.loop(early, tiles // 2)(pick)
    inv_hi = jnp.concatenate([sel[0, pl.ds(0, mb)], sel[0, pl.ds(mb, mb)]], axis=1).astype(BF16)
    inv_lo = jnp.concatenate([sel[1, pl.ds(0, mb)], sel[1, pl.ds(mb, mb)]], axis=1).astype(BF16)

    await_bytes(gath.at[pl.ds(0, 2 * nz - 1)], ga_r)
    rows = gath[...].reshape(nq, LANES)
    part = three_pass(inv_hi, inv_lo, jnp.concatenate([rows, turned(rows)], axis=0))
    vpart[...] = part.reshape(vpart.shape)

    for d in far_first(ny):
        remote(vpart.at[(y + d) % ny], rpart.at[y], sent_sem, rs_r, along_y(d), col).start()
    rpart[y] = vpart[y]

    away = (4, 3, 5, 2, 6, 1, 7, 0)

    def split_panel(src, lane):
        for n in range(nz):
            at = pl.ds(n * tb, tb)
            for c in range(2):
                hi, lo = split(src[(z + away[n]) % nz, pl.ds(c, tb, 2), :])
                lhs_hi[at, pl.ds(lane + c * LANES, LANES)] = hi
                lhs_lo[at, pl.ds(lane + c * LANES, LANES)] = lo

    loads[3].wait()
    split_panel(pown, 0)
    if ny > 1:
        await_bytes(rpart.at[pl.ds(0, ny - 1)], rs_r)
    sol[row] = functools.reduce(lambda a, b: a + b, [rpart[n] for n in range(ny)])

    plane = sorted(
        [(dx, dy) for dx in range(NX) for dy in range(ny) if dx or dy],
        key=lambda at: (min(at[0], NX - at[0]), -min(at[1], ny - at[1])),
    )
    for dx, dy in plane:
        to_row = ((x + dx) % NX) * ny + (y + dy) % ny
        remote(sol.at[row], sol.at[row], sent_sem, s_r.at[x], to_row, col).start()
    pshare = remote(pc_in.at[:, 1 - core], psib, p_s, p_r, row, other)
    pshare.start()

    pshare.wait_recv()
    split_panel(psib, 2 * LANES)

    def pass_on(k):
        s = (x + order[k]) % NX
        line = pl.ds(s * ny, ny)
        if k > 0:
            await_bytes(sol.at[line], s_r.at[s])
        elif ny > 1:
            await_bytes(sol.at[pl.ds(s * ny, ny - 1)], s_r.at[s])
        copy = remote(sol.at[line], sib.at[line], sent_sem, t_r.at[k], row, other)
        copy.start()
        return copy

    order = (0, 1, 3, 2)

    def leg(k, direction, slot):
        sign = 1 - 2 * direction
        block = (0, 1, 3, 5)[slot] + (direction if slot else 0)
        at = pl.ds(direction * (tb // 2), tb // 2) if slot == 0 else pl.ds(0, tb)
        return at, remote(
            prod.at[k, block, at], arrive.at[k, direction, slot, at],
            sent_sem, ring_r.at[k, direction, max(slot, 1) - 1], row, along_z(sign * (1 if slot else 2)),
        )

    def came(k, direction, slot):
        if slot == 1:
            await_bytes(arrive.at[k, direction, pl.ds(0, 2), pl.ds(0, tb * 3 // 4)], ring_r.at[k, direction, 0])
        else:
            await_bytes(arrive.at[k, direction, slot], ring_r.at[k, direction, slot - 1])

    def advance(k, slot):
        for direction in range(2):
            if slot > 1:
                came(k, direction, slot - 1)
                block = (0, 1, 3, 5)[slot] + direction
                prod[k, block] += arrive[k, direction, slot - 1]
                if slot == 2:
                    at = leg(k, direction, 0)[0]
                    prod[k, block, at] += arrive[k, direction, 0, at]
            leg(k, direction, slot)[1].start()

    def finish(k):
        result = prod[k, 7]
        for direction in range(2):
            came(k, direction, 3)
            result = result + arrive[k, direction, 3]
        s = (x + order[k]) % NX
        swapped = swap_halves(result)
        first = s % 2 == 0
        mine = left_lanes(result.shape) == first
        for c, values in enumerate((
            jnp.where(first, result, swapped), jnp.where(first, swapped, result)
        )):
            at = pl.ds(2 * (s // 2) + c, tb, 4)
            upd_v[at, :] -= jnp.where(mine, values, 0.0)

    def slice_rows(ref, s):
        return ref[pl.ds(s * ny, ny)].reshape(mb, LANES)

    def panel_rhs(k):
        s = (x + order[k]) % NX
        passed[k].wait_recv()
        own, sibling = slice_rows(sol, s), slice_rows(sib, s)
        return jnp.concatenate([own, turned(own), sibling, turned(sibling)], axis=0)

    def product(k, rhs, first, count):
        at = pl.ds(first * tb, count * tb)
        block = three_pass(lhs_hi[at, :], lhs_lo[at, :], rhs)
        prod[k, pl.ds(first, count)] = block.reshape(count, tb, LANES)

    def unpack(first, second):
        mask = left_lanes(first.shape)
        return (
            jnp.where(mask, first, swap_halves(second)),
            jnp.where(mask, swap_halves(first), second),
        )

    adj_copy = pltpu.make_async_copy(adj_v, adj_out, out_sem.at[0])

    def panel_results():
        loads[4].wait()
        for t in range(2):
            parts = unpack(slice_rows(sol, 2 * t), slice_rows(sol, 2 * t + 1))
            acc = None
            for c in range(2):
                at = pl.ds(2 * t + c, mb, 4)
                adj_v[at, :] = parts[c]
                term = parts[c] * de_v[at, :]
                acc = term if acc is None else acc + term
            sens_v[z, pl.ds(t, 1)] = -jnp.sum(acc, axis=0, keepdims=True)
        for d in far_first(nz):
            remote(sens_v.at[z], sens_v.at[z], sent_sem, u_r, row, along_z(d)).start()
        adj_copy.start()

    passed = [pass_on(0)]
    rhs = []

    def lead(k):
        rhs.append(panel_rhs(k))
        product(k, rhs[k], 0, 3)
        advance(k, 0)
        advance(k, 1)

    def trail(k):
        product(k, rhs[k], 3, 5)

    lead(0)
    trail(0)
    passed += [pass_on(1), pass_on(2)]
    lead(1)
    lead(2)
    passed.append(pass_on(3))
    trail(1)
    trail(2)
    lead(3)
    advance(0, 2)
    trail(3)
    panel_results()
    for k in range(1, NX):
        advance(k, 2)
    for k in range(NX):
        advance(k, 3)
    await_bytes(sens_v.at[pl.ds(0, nz - 1)], u_r)
    sens_o[...] = functools.reduce(lambda a, b: a + b, [sens_v[n] for n in range(nz)])
    sens_hand = remote(sens_o, sens_x, sent_sem, ux_r, row, other)
    sens_hand.start()
    loads[5].wait()
    for k in range(NX):
        finish(k)

    upd_copy = pltpu.make_async_copy(upd_v, upd_out, out_sem.at[1])
    upd_copy.start()
    sens_hand.wait_recv()
    sens_x[...] += sens_o[...]
    sens_copy = pltpu.make_async_copy(sens_x, sens_out, out_sem.at[2])
    sens_copy.start()

    pshare.wait_send()
    piece = mb // ny
    sent = (
        (NX - 1) * hsend.shape[1] + (2 * nz - 1) * NX * rpd + (ny - 1) * piece + (NX * ny - 1) * piece
        + NX * mb + NX * (nz - 1) * tb + (nz - 1) * 2 + 2
    )
    await_bytes(dinv_v.at[pl.ds(0, sent)], sent_sem)
    adj_copy.wait()
    upd_copy.wait()
    sens_copy.wait()


def place(*refs):
    count = len(refs) // 2
    sems = refs[-1]
    copies = [
        pltpu.make_async_copy(refs[n], refs[count + n], sems.at[n]) for n in range(count)
    ]
    for copy in copies:
        copy.start()
    for copy in copies:
        copy.wait()


def rows_of_lanes(array):
    count, parts, width = array.shape
    tiles = width // LANES
    array = array.reshape(count, parts, tiles, LANES).transpose(0, 2, 1, 3)
    return array.reshape(count * tiles * parts, LANES)


def from_rows(array, count, tiles):
    return array.reshape(count, tiles, 2, LANES).transpose(0, 2, 1, 3).reshape(count, 2, tiles * LANES)


def make_per_device(prow, pcol):
    ny, nz = prow // NX, pcol // 2

    def per_device(rhs_panel, pivots, diag_inverse, panel_column, trailing, derivative):
        rpd = rhs_panel.shape[0]
        mb = diag_inverse.shape[0]
        tb = trailing.shape[0]
        nb = pivots.shape[0]
        vmem = lambda *shape: pltpu.VMEM(shape, F32)
        half = lambda *shape: pltpu.VMEM(shape, BF16)
        dma = lambda *shape: pltpu.SemaphoreType.DMA(shape) if shape else pltpu.SemaphoreType.DMA
        pad = -(-rpd // 8) * 8
        scratch = [
            vmem(rpd * 4, LANES), vmem(rpd * 4, LANES), pltpu.VMEM((nb // LANES, LANES), jnp.int32),
            vmem(mb * 2 * (nb // LANES), LANES),
            vmem(nz, 2 * tb, LANES), vmem(nz, 2 * tb, LANES),
            vmem(mb * 4, LANES),
            vmem(NX, pad, LANES), vmem(NX, pad, LANES), vmem(pcol, NX * rpd, LANES),
            vmem(2, 2 * mb, pcol * NX * rpd),
            vmem(ny, mb // ny, LANES), vmem(ny, mb // ny, LANES),
            vmem(NX * ny, mb // ny, LANES), vmem(NX * ny, mb // ny, LANES),
            half(nz * tb, 4 * LANES), half(nz * tb, 4 * LANES),
            vmem(NX, nz, tb, LANES), vmem(NX, 2, 4, tb, LANES),
            vmem(tb * 4, LANES), vmem(mb * 4, LANES), vmem(nz, 2, LANES), vmem(2, LANES), vmem(2, LANES),
            dma(6), dma(3), dma(), dma(), dma(), dma(NX), dma(NX), dma(), dma(), dma(NX, 2, 3), dma(), dma(), dma(),
        ]
        anywhere = pl.BlockSpec(memory_space=pltpu.HBM)
        updated, solved, sens = pl.pallas_call(
            functools.partial(kernel, ny, nz, rpd),
            out_shape=(
                jax.ShapeDtypeStruct((tb * 4, LANES), F32),
                jax.ShapeDtypeStruct((mb * 4, LANES), F32),
                jax.ShapeDtypeStruct((2, LANES), F32),
            ),
            in_specs=[anywhere] * 6,
            out_specs=(anywhere,) * 3,
            scratch_shapes=scratch,
            compiler_params=pltpu.CompilerParams(
                collective_id=0, has_side_effects=True, vmem_limit_bytes=48 * 1024 * 1024
            ),
            name="panel_step",
        )(*[pltpu.with_memory_space_constraint(operand, pltpu.HBM) for operand in (
            rows_of_lanes(rhs_panel),
            pivots.reshape(nb // LANES, LANES),
            rows_of_lanes(diag_inverse),
            rows_of_lanes(panel_column).reshape(nz, 2, 2 * tb, LANES),
            rows_of_lanes(trailing),
            rows_of_lanes(derivative),
        )])
        updated, solved, sens = pl.pallas_call(
            place,
            out_shape=(
                jax.ShapeDtypeStruct(updated.shape, F32),
                jax.ShapeDtypeStruct(solved.shape, F32),
                jax.ShapeDtypeStruct(sens.shape, F32),
            ),
            in_specs=[pl.BlockSpec(memory_space=pltpu.VMEM)] * 3,
            out_specs=(pl.BlockSpec(memory_space=pltpu.HBM),) * 3,
            scratch_shapes=[pltpu.SemaphoreType.DMA((3,))],
            name="place_results",
        )(*[
            pltpu.with_memory_space_constraint(result, pltpu.VMEM)
            for result in (updated, solved, sens)
        ])
        return from_rows(updated, tb, 2), from_rows(solved, mb, 2), sens.reshape(2 * LANES)

    return per_device


def solution(mesh):
    in_specs = (
        P(("prow", "pcol"), None, None),
        P(),
        P("pcol", None, None),
        P("prow", None, "pcol"),
        P(("prow", "pcol"), None, None),
        P("pcol", None, None),
    )
    out_specs = (P(("prow", "pcol"), None, None), P("pcol", None, None), P())
    per_device = make_per_device(mesh.shape["prow"], mesh.shape["pcol"])
    return jax.shard_map(
        per_device, mesh=mesh, in_specs=in_specs, out_specs=out_specs, check_vma=False
    )
```
